128 devices in a mesh: dp: 4 (over x), seq: 32 (over y, z, core).
Axes of the slice: x: 4, y: 4, z: 4, core: 2. Of those that a mesh axis runs over, the one named last changes fastest.
Arguments:
- tokens: bfloat16 [4, 16384, 1024], P('dp', 'seq'), may hold values from -6 to 6
- w_query: bfloat16 [1024, 1024], replicated, may hold values from -0.1875 to 0.1875
- w_key: bfloat16 [1024, 1024], replicated, may hold values from -0.1875 to 0.1875
- w_value: bfloat16 [1024, 1024], replicated, may hold values from -0.1875 to 0.1875
- proj_keys: bfloat16 [256, 16384], P(None, 'seq'), may hold values from -0.1875 to 0.1875
- proj_values: bfloat16 [256, 16384], P(None, 'seq'), may hold values from -0.1875 to 0.1875
- grad_out: bfloat16 [4, 16384, 1024], P('dp', 'seq'), may hold values from -6 to 6
Outputs:
- attended: bfloat16 [4, 16384, 1024], P('dp', 'seq')
- grad_tokens: bfloat16 [4, 16384, 1024], P('dp', 'seq')
- weight_grads: float32 [1024, 3072], P(('dp', 'seq'))
The draws below stay inside these ranges and needn't reach their ends.
All inputs are finite; a program needn't handle non-finite values.
Results may differ from the reference program's by a relative error of at most 0.013.
The reference program's roundings to bfloat16 on the way (of `query`, `probs_low`, `dscores` and `grad_query`) count: a program that leaves them out, or rounds other values in their place, can miss the bound.
Values sent between devices are 32-bit elements; how exact they have to be, the bound alone decides.
No kernel may reach another device: no remote copies, remote signals or barrier semaphores. Data moves between devices by JAX's collectives and lax.ppermute only.
A program may use at most 128 MiB of HBM per device.

```python
import jax
import jax.numpy as jnp
from jax import lax

D = 1024
HEADS = 16
HEAD_DIM = 64
PROJ = 256
LENGTH = 16384
DOCS = 4


def with_spikes(entries, own_key, source, target, blocks, factor):
    owner, partner = [(jnp.arange(entries.shape[position]) // (entries.shape[position] // blocks)).reshape([-1 if axis == position else 1 for axis in range(entries.ndim)]) for position in (source, target)]
    chosen = jax.random.permutation(own_key, blocks)[partner]
    strong = (owner == chosen) | (owner == (partner + blocks // 2) % blocks)
    return jnp.where(strong, factor * entries, entries)


def block_levels(key, extent, cuts, smallest, largest):
    loudness, own = 1.0, jax.random.fold_in(key, 6)
    for axis_at, blocks in cuts:
        steps = jnp.exp(jax.random.uniform(jax.random.fold_in(own, axis_at), (blocks,), jnp.float32, smallest / len(cuts), largest / len(cuts)))
        loudness = loudness * jnp.repeat(steps, extent[axis_at] // blocks).reshape([-1 if axis == axis_at else 1 for axis in range(len(extent))])
    return loudness


def normal_values(rng, extent, deviation, limit, pieces=(), kind=jnp.bfloat16):
    array = jax.random.normal(rng, extent, jnp.float32) * deviation
    if len(pieces) > 0:
        array = block_levels(rng, extent, pieces, -0.22, 0.18) * array
    return jnp.clip(array, min=-limit, max=limit).astype(kind)


def noise_with(own_key, dims, spread, most, pieces, heavy, held_as=jnp.bfloat16):
    result = spread * jax.random.normal(own_key, dims, jnp.float32)
    if pieces:
        result = result * block_levels(own_key, dims, pieces, -0.22, 0.18)
    return jnp.clip(with_spikes(result, jax.random.fold_in(own_key, 3), *heavy), -most, most).astype(held_as)


def setup_inputs(seed: int = 0) -> dict:
    arg_keys = jax.random.split(jax.random.key(seed), 8)
    return {
        "tokens": noise_with(arg_keys[0], (DOCS, LENGTH, D), 1.0, 6.0, ((0, 4), (1, 32)), (1, 2, 32, 2.75)),
        "w_query": normal_values(arg_keys[1], (D, D), D ** -0.5, 0.1875),
        "w_key": normal_values(arg_keys[2], (D, D), D ** -0.5, 0.1875),
        "w_value": normal_values(arg_keys[3], (D, D), D ** -0.5, 0.1875),
        "proj_keys": normal_values(arg_keys[4], (PROJ, LENGTH), (LENGTH // 16) ** -0.5, 0.1875, ((1, 32),)),
        "proj_values": normal_values(arg_keys[5], (PROJ, LENGTH), (LENGTH // 16) ** -0.5, 0.1875, ((1, 32),)),
        "grad_out": normal_values(arg_keys[6], (DOCS, LENGTH, D), 1.0, 6.0, ((0, 4), (1, 32))),
    }


def exact_dot(left, right):
    return jnp.dot(left, right, preferred_element_type=jnp.float32, precision=lax.Precision.HIGHEST)

def one_document(tokens, w_query, w_key, w_value, proj_keys, proj_values, grad_out):
    key_weight = w_key.astype(jnp.float32)
    value_weight = w_value.astype(jnp.float32)
    query = jnp.dot(tokens, w_query, preferred_element_type=jnp.float32).astype(jnp.bfloat16)
    key_tokens = jnp.dot(proj_keys, tokens, preferred_element_type=jnp.float32)
    value_tokens = jnp.dot(proj_values, tokens, preferred_element_type=jnp.float32)
    key_proj = exact_dot(key_tokens, key_weight).astype(jnp.bfloat16)
    value_proj = exact_dot(value_tokens, value_weight).astype(jnp.bfloat16)
    query_h = query.astype(jnp.float32).reshape(LENGTH, HEADS, HEAD_DIM)
    key_h = key_proj.astype(jnp.float32).reshape(PROJ, HEADS, HEAD_DIM)
    value_h = value_proj.astype(jnp.float32).reshape(PROJ, HEADS, HEAD_DIM)
    grad_h = grad_out.astype(jnp.float32).reshape(LENGTH, HEADS, HEAD_DIM)
    scores = jnp.einsum('shd,phd->hsp', query_h, key_h) * 0.125
    probs = jax.nn.softmax(scores, axis=-1)
    probs_low = probs.astype(jnp.bfloat16).astype(jnp.float32)
    attended = jnp.einsum('hsp,phd->shd', probs_low, value_h).astype(jnp.bfloat16).reshape(LENGTH, D)
    dprobs = jnp.einsum('shd,phd->hsp', grad_h, value_h)
    dscores = (probs * (dprobs - lax.optimization_barrier(jnp.sum(dprobs * probs, axis=-1, keepdims=True))) * 0.125).astype(jnp.bfloat16).astype(jnp.float32)
    grad_query = jnp.einsum('hsp,phd->shd', dscores, key_h).astype(jnp.bfloat16).reshape(LENGTH, D)
    grad_key_proj = jnp.einsum('hsp,shd->phd', dscores, query_h).reshape(PROJ, D)
    grad_value_proj = jnp.einsum('hsp,shd->phd', probs_low, grad_h).reshape(PROJ, D)
    grad_key_tokens = exact_dot(grad_key_proj, key_weight.T).astype(jnp.bfloat16)
    grad_value_tokens = exact_dot(grad_value_proj, value_weight.T).astype(jnp.bfloat16)
    grad_tokens = jnp.dot(grad_query, w_query.T, preferred_element_type=jnp.float32)
    grad_tokens = grad_tokens + jnp.dot(proj_keys.T, grad_key_tokens, preferred_element_type=jnp.float32)
    grad_tokens = grad_tokens + jnp.dot(proj_values.T, grad_value_tokens, preferred_element_type=jnp.float32)
    grad_tokens = grad_tokens.astype(jnp.bfloat16)
    grads = jnp.concatenate([jnp.dot(tokens.T, grad_query, preferred_element_type=jnp.float32), exact_dot(key_tokens.T, grad_key_proj), exact_dot(value_tokens.T, grad_value_proj)], axis=1)
    return (attended, grad_tokens, grads)

def reference(tokens, w_query, w_key, w_value, proj_keys, proj_values, grad_out):
    attended_all = []
    grad_all = []
    grads = jnp.zeros((D, 3 * D), jnp.float32)
    for index in range(DOCS):
        attended, grad_tokens, term = one_document(tokens[index], w_query, w_key, w_value, proj_keys, proj_values, grad_out[index])
        attended_all.append(attended)
        grad_all.append(grad_tokens)
        grads = grads + term
    clip = jnp.minimum(1.0, lax.rsqrt(jnp.sum(grads * grads) + 1e-06))
    return (jnp.stack(attended_all), jnp.stack(grad_all), grads * clip)
```

```python
import jax
import jax.numpy as jnp
from jax import lax
from jax.experimental import pallas as pl
from jax.experimental.pallas import tpu as pltpu
from jax.sharding import PartitionSpec as P

D = 1024
HEADS = 16
HEAD_DIM = 64
PROJ = 256
DP = 4
CHIPS = 16
SEQ = "seq"
F32 = jnp.float32
BF16 = jnp.bfloat16
LOG2E = 1.4426950408889634


def place(y, z, core):
    return ((y % 4) * 4 + z % 4) * 2 + core % 2


def moved(dy, dz, dcore):
    return [
        (place(y, z, c), place(y + dy, z + dz, c + dcore))
        for y in range(4)
        for z in range(4)
        for c in range(2)
    ]


SAME_CORE = [[2 * chip + core for chip in range(CHIPS)] for core in range(2)]


def swap_cores(x):
    return lax.ppermute(x, SEQ, moved(0, 0, 1))


def along_x(x, step):
    return lax.ppermute(x, "dp", [(d, (d + step) % DP) for d in range(DP)])


def exchange_chips(x):
    return lax.all_to_all(x, SEQ, 0, 0, axis_index_groups=SAME_CORE)


def scatter_sum(x):
    return jnp.sum(exchange_chips(x.reshape(CHIPS, x.shape[0] // CHIPS, x.shape[1])), axis=0)


def gather_rows(x):
    rows = exchange_chips(jnp.broadcast_to(x[None], (CHIPS, *x.shape)))
    return rows.reshape(CHIPS * x.shape[0], x.shape[1])


def dot_f32(form, left, right, precision=None):
    return jnp.einsum(form, left, right, preferred_element_type=F32, precision=precision)


def mm(left, right, left_dim, right_dim):
    return lax.dot_general(
        left, right, (((left_dim,), (right_dim,)), ((), ())), preferred_element_type=F32
    )


def attention_kernel(query_ref, grad_ref, key_ref, value_ref, att_ref, gq_ref, gk_ref, gv_ref):
    att, gq, gk, gv = [], [], [], []
    for h in range(2):
        rows = pl.ds(h * HEAD_DIM, HEAD_DIM)
        query, grad = query_ref[rows, :], grad_ref[rows, :]
        key, value = key_ref[rows, :].astype(BF16), value_ref[rows, :].astype(BF16)
        scores = mm(key, query, 0, 0)
        top = jnp.max(scores, axis=0, keepdims=True)
        raised = jnp.exp2((scores - top) * (0.125 * LOG2E))
        probs = raised * (1.0 / jnp.sum(raised, axis=0, keepdims=True))
        low = probs.astype(BF16)
        dprobs = mm(value, grad, 0, 0)
        inner = jnp.sum(dprobs * probs, axis=0, keepdims=True)
        dscores = (probs * (dprobs - inner) * 0.125).astype(BF16)
        att.append(mm(value, low, 1, 0))
        gq.append(mm(key, dscores, 1, 0))
        gk.append(mm(dscores, query, 1, 1))
        gv.append(mm(low, grad, 1, 1))
    att_ref[...] = jnp.concatenate(att, axis=0).T.astype(BF16)
    gq_ref[...] = jnp.concatenate(gq, axis=0).T.astype(BF16)
    gk_ref[...] = jnp.concatenate(gk, axis=1)
    gv_ref[...] = jnp.concatenate(gv, axis=1)


def attention(query_t, grad_t, key_t, value_t):
    length = query_t.shape[1]
    wide = pl.BlockSpec((2 * HEAD_DIM, length), lambda i: (i, 0))
    narrow = pl.BlockSpec((2 * HEAD_DIM, PROJ), lambda i: (i, 0))
    return pl.pallas_call(
        attention_kernel,
        grid=(HEADS // 2,),
        in_specs=[wide, wide, narrow, narrow],
        out_specs=[
            pl.BlockSpec((length, 2 * HEAD_DIM), lambda i: (0, i)),
            pl.BlockSpec((length, 2 * HEAD_DIM), lambda i: (0, i)),
            pl.BlockSpec((PROJ, 2 * HEAD_DIM), lambda i: (0, i)),
            pl.BlockSpec((PROJ, 2 * HEAD_DIM), lambda i: (0, i)),
        ],
        out_shape=[
            jax.ShapeDtypeStruct((length, D), BF16),
            jax.ShapeDtypeStruct((length, D), BF16),
            jax.ShapeDtypeStruct((PROJ, D), F32),
            jax.ShapeDtypeStruct((PROJ, D), F32),
        ],
        compiler_params=pltpu.CompilerParams(vmem_limit_bytes=48 * 1024 * 1024),
        cost_estimate=pl.CostEstimate(
            flops=12 * length * PROJ * D, bytes_accessed=8 * 1024 * 1024, transcendentals=length * PROJ * HEADS
        ),
        name="attention",
    )(query_t, grad_t, key_t, value_t)


def grad_tokens_kernel(first_ref, pk_ref, pv_ref, gk_ref, gv_ref, out_ref):
    total = first_ref[...]
    total += mm(pk_ref[...], gk_ref[...].astype(BF16), 0, 0)
    total += mm(pv_ref[...], gv_ref[...].astype(BF16), 0, 0)
    out_ref[...] = total.astype(BF16)


def finish_tokens(first, proj_keys, proj_values, gk_tokens, gv_tokens):
    length = first.shape[0]
    tile = 256
    column = lambda rows: pl.BlockSpec((rows, tile), lambda i: (0, i))
    whole = pl.BlockSpec((PROJ, length), lambda i: (0, 0))
    return pl.pallas_call(
        grad_tokens_kernel,
        grid=(D // tile,),
        in_specs=[column(length), whole, whole, column(PROJ), column(PROJ)],
        out_specs=column(length),
        out_shape=jax.ShapeDtypeStruct((length, D), BF16),
        compiler_params=pltpu.CompilerParams(vmem_limit_bytes=48 * 1024 * 1024),
        cost_estimate=pl.CostEstimate(
            flops=4 * length * PROJ * D, bytes_accessed=6 * 1024 * 1024, transcendentals=0
        ),
        name="grad_tokens",
    )(first, proj_keys, proj_values, gk_tokens, gv_tokens)


def sum_everywhere(x):
    x = x + swap_cores(x)
    x = x + sum(lax.ppermute(x, SEQ, moved(0, k, 0)) for k in (1, 2, 3))
    x = x + sum(lax.ppermute(x, SEQ, moved(k, 0, 0)) for k in (1, 2, 3))
    return x + sum(along_x(x, k) for k in (1, 2, 3))


def per_device(tokens, w_query, w_key, w_value, proj_keys, proj_values, grad_out):
    inputs = tokens[0]
    upstream = grad_out[0]
    seq_place = lax.axis_index(SEQ)
    chip, core = seq_place // 2, seq_place % 2
    dp_place = lax.axis_index("dp")
    first_core = core == 0
    exact = lax.Precision.HIGHEST

    theirs = jnp.where(first_core, proj_values, proj_keys)
    ours = jnp.where(first_core, proj_keys, proj_values)
    my_weight = jnp.where(first_core, w_key, w_value).astype(F32)
    arrived = swap_cores(dot_f32("ps,sd->pd", theirs, inputs))
    part = dot_f32("ps,sd->pd", ours, inputs) + arrived
    my_tokens = gather_rows(scatter_sum(part))
    my_proj_t = dot_f32("pe,ed->dp", my_tokens, my_weight, exact)
    other_proj_t = swap_cores(my_proj_t)
    key_t = jnp.where(first_core, my_proj_t, other_proj_t)
    value_t = jnp.where(first_core, other_proj_t, my_proj_t)

    query_t = dot_f32("sd,de->es", inputs, w_query).astype(BF16)
    attended, grad_query, gk_part, gv_part = attention(query_t, upstream.T, key_t, value_t)

    arrived = swap_cores(jnp.where(first_core, gv_part, gk_part))
    part = jnp.where(first_core, gk_part, gv_part) + arrived
    my_grad = gather_rows(scatter_sum(part))
    my_grad_tokens = dot_f32("pe,de->pd", my_grad, my_weight, exact)
    other_grad_tokens = swap_cores(my_grad_tokens)
    gk_tokens = jnp.where(first_core, my_grad_tokens, other_grad_tokens)
    gv_tokens = jnp.where(first_core, other_grad_tokens, my_grad_tokens)
    direct = dot_f32("se,de->sd", grad_query, w_query)
    grad_tokens = finish_tokens(direct, proj_keys, proj_values, gk_tokens, gv_tokens)

    rows = D // (DP * CHIPS * 2)
    wq = dot_f32("sc,se->ce", inputs, grad_query).reshape(DP, CHIPS, 2, rows, D)
    arrived = swap_cores(lax.dynamic_index_in_dim(wq, 1 - core, 2, keepdims=False))
    wq = lax.dynamic_index_in_dim(wq, core, 2, keepdims=False) + arrived
    at = lambda k: lax.dynamic_index_in_dim(wq, (dp_place + k) % DP, 0, keepdims=False)
    far, half = at(2), CHIPS // 2
    up, down = along_x(far[:half], 1), along_x(far[half:], -1)
    ahead, behind = at(1), at(3)
    ahead = jnp.concatenate([ahead[:half] + up, ahead[half:]], axis=0)
    behind = jnp.concatenate([behind[:half], behind[half:] + down], axis=0)
    wq = at(0) + along_x(ahead, 1) + along_x(behind, -1)
    wq = jnp.sum(exchange_chips(wq), axis=0)

    columns = lax.dynamic_index_in_dim(my_tokens.reshape(PROJ, DP, CHIPS, 2 * rows), chip, 2, keepdims=False)
    wkv = dot_f32("pdr,pe->dre", columns, my_grad, exact)
    quarter = lambda k: lax.dynamic_index_in_dim(wkv, (dp_place + k) % DP, 0, keepdims=False)
    wkv = quarter(0) + along_x(quarter(1), 1) + along_x(quarter(2), 2) + along_x(quarter(3), 3)
    wkv = wkv.reshape(2, rows, D)
    arrived = swap_cores(lax.dynamic_index_in_dim(wkv, 1 - core, 0, keepdims=False))
    mine = lax.dynamic_index_in_dim(wkv, core, 0, keepdims=False)
    wk = jnp.where(first_core, mine, arrived)
    wv = jnp.where(first_core, arrived, mine)
    grads = jnp.concatenate([wq, wk, wv], axis=1)
    squared = sum_everywhere(jnp.full((8, 128), jnp.sum(grads * grads)))[0, 0]
    clip = jnp.minimum(1.0, lax.rsqrt(squared + 1e-06))
    return (attended[None], grad_tokens[None], grads * clip)


def solution(mesh):
    return jax.shard_map(
        per_device,
        mesh=mesh,
        in_specs=(
            P("dp", "seq", None),
            P(),
            P(),
            P(),
            P(None, "seq"),
            P(None, "seq"),
            P("dp", "seq", None),
        ),
        out_specs=(P("dp", "seq", None), P("dp", "seq", None), P(("dp", "seq"), None)),
        check_vma=False,
    )
```

```python
import functools

import jax
import jax.numpy as jnp
from jax import lax
from jax.experimental import pallas as pl
from jax.experimental.pallas import tpu as pltpu
from jax.sharding import PartitionSpec as P

D = 1024
HEADS = 16
HEAD_DIM = 64
PROJ = 256
DP = 4
CHIPS = 16
SEQ = "seq"
F32 = jnp.float32
BF16 = jnp.bfloat16
GROUP = 4
LOG2E = 1.4426950408889634


def place(y, z, core):
    return ((y % 4) * 4 + z % 4) * 2 + core % 2


def moved(dy, dz, dcore):
    return [
        (place(y, z, c), place(y + dy, z + dz, c + dcore))
        for y in range(4)
        for z in range(4)
        for c in range(2)
    ]


SAME_CORE = [[2 * chip + core for chip in range(CHIPS)] for core in range(2)]


def swap_cores(x):
    return lax.ppermute(x, SEQ, moved(0, 0, 1))


def along_x(x, step):
    return lax.ppermute(x, "dp", [(d, (d + step) % DP) for d in range(DP)])


def exchange_chips(x):
    return lax.all_to_all(x, SEQ, 0, 0, axis_index_groups=SAME_CORE)


def beside(x, *others):
    return lax.optimization_barrier((x, *others))


def scatter_rows(x):
    return exchange_chips(x.reshape(CHIPS, x.shape[0] // CHIPS, x.shape[1]))


def gather_sum(raw):
    copies = sum_copies(raw)
    rows = exchange_chips(copies)
    return rows.reshape(raw.shape[0] * raw.shape[1], raw.shape[2])


def dot_f32(form, left, right, precision=None):
    return jnp.einsum(form, left, right, preferred_element_type=F32, precision=precision)


def mm(left, right, left_dim, right_dim):
    return lax.dot_general(
        left, right, (((left_dim,), (right_dim,)), ((), ())), preferred_element_type=F32
    )


def attention_kernel(core_ref, query_ref, grad_ref, mine_ref, other_ref, att_ref, gq_ref, ours_ref, theirs_ref):
    first_core = core_ref[0] == 0
    mine, other = mine_ref[...], other_ref[...]
    keys = jnp.where(first_core, mine, other).astype(BF16)
    values = jnp.where(first_core, other, mine).astype(BF16)
    att, gq, gk, gv = [], [], [], []
    for h in range(GROUP):
        rows = slice(h * HEAD_DIM, (h + 1) * HEAD_DIM)
        query, grad, key, value = query_ref[rows, :], grad_ref[rows, :], keys[rows], values[rows]
        scores = mm(key, query, 0, 0)
        top = jnp.max(scores, axis=0, keepdims=True)
        raised = jnp.exp2((scores - top) * (0.125 * LOG2E))
        probs = raised * (1.0 / jnp.sum(raised, axis=0, keepdims=True))
        low = probs.astype(BF16)
        dprobs = mm(value * BF16(0.125), grad, 0, 0)
        inner = jnp.sum(dprobs * probs, axis=0, keepdims=True)
        dscores = (probs * (dprobs - inner)).astype(BF16)
        att.append(mm(value, low, 1, 0))
        gq.append(mm(key, dscores, 1, 0))
        gk.append(mm(query, dscores, 1, 1))
        gv.append(mm(grad, low, 1, 1))
    att_ref[...] = jnp.concatenate(att, axis=0).T.astype(BF16)
    gq_ref[...] = jnp.concatenate(gq, axis=0).T.astype(BF16)
    gk, gv = jnp.concatenate(gk, axis=0), jnp.concatenate(gv, axis=0)
    ours_ref[...] = jnp.where(first_core, gk, gv)
    theirs_ref[...] = jnp.where(first_core, gv, gk)


def attention(core, query_t, grad_t, mine_t, other_t):
    length = query_t.shape[1]
    wide = pl.BlockSpec((GROUP * HEAD_DIM, length), lambda i: (i, 0))
    narrow = pl.BlockSpec((GROUP * HEAD_DIM, PROJ), lambda i: (i, 0))
    tall = pl.BlockSpec((length, GROUP * HEAD_DIM), lambda i: (0, i))
    return pl.pallas_call(
        attention_kernel,
        grid=(HEADS // GROUP,),
        in_specs=[pl.BlockSpec(memory_space=pltpu.SMEM), wide, wide, narrow, narrow],
        out_specs=[tall, tall, narrow, narrow],
        out_shape=[
            jax.ShapeDtypeStruct((length, D), BF16),
            jax.ShapeDtypeStruct((length, D), BF16),
            jax.ShapeDtypeStruct((D, PROJ), F32),
            jax.ShapeDtypeStruct((D, PROJ), F32),
        ],
        compiler_params=pltpu.CompilerParams(vmem_limit_bytes=48 * 1024 * 1024),
        cost_estimate=pl.CostEstimate(
            flops=12 * length * PROJ * D, bytes_accessed=8 * 1024 * 1024, transcendentals=length * PROJ * HEADS
        ),
        name="attention",
    )(core, query_t, grad_t, mine_t, other_t)


def sum_copies_kernel(x_ref, out_ref):
    total = x_ref[0]
    for chip in range(1, CHIPS):
        total += x_ref[chip]
    for chip in range(CHIPS):
        out_ref[chip] = total


def sum_copies(x):
    return pl.pallas_call(
        sum_copies_kernel,
        out_shape=jax.ShapeDtypeStruct(x.shape, F32),
        cost_estimate=pl.CostEstimate(flops=x.size, bytes_accessed=8 * x.size, transcendentals=0),
        compiler_params=pltpu.CompilerParams(vmem_limit_bytes=32 * 1024 * 1024),
        name="sum_copies",
    )(x)


def grad_tokens_kernel(core_ref, first_ref, pk_ref, pv_ref, mine_ref, other_ref, out_ref):
    first_core = core_ref[0] == 0
    mine, other = mine_ref[...], other_ref[...]
    gk = jnp.where(first_core, mine, other).astype(BF16)
    gv = jnp.where(first_core, other, mine).astype(BF16)
    total = first_ref[...]
    total += mm(pk_ref[...], gk, 1, 1)
    total += mm(pv_ref[...], gv, 1, 1)
    out_ref[...] = total.astype(BF16)


def finish_tokens(core, first, pk_t, pv_t, mine_t, other_t):
    length = first.shape[0]
    tile = 256
    column = pl.BlockSpec((length, tile), lambda i: (0, i))
    row = pl.BlockSpec((tile, PROJ), lambda i: (i, 0))
    whole = pl.BlockSpec((length, PROJ), lambda i: (0, 0))
    return pl.pallas_call(
        grad_tokens_kernel,
        grid=(D // tile,),
        in_specs=[pl.BlockSpec(memory_space=pltpu.SMEM), column, whole, whole, row, row],
        out_specs=column,
        out_shape=jax.ShapeDtypeStruct((length, D), BF16),
        compiler_params=pltpu.CompilerParams(vmem_limit_bytes=32 * 1024 * 1024),
        cost_estimate=pl.CostEstimate(
            flops=1, bytes_accessed=1, transcendentals=0
        ),
        name="grad_tokens",
    )(core, first, pk_t, pv_t, mine_t, other_t)


def exchange_x(x):
    return lax.all_to_all(x, "dp", 0, 0)


def finish_sums_kernel(raw_ref, wkv_ref, wq_ref, squares_ref):
    total = raw_ref[0]
    for chip in range(1, CHIPS):
        total += raw_ref[chip]
    wq_ref[...] = total
    wkv = wkv_ref[...]
    rows = total.shape[0]
    squared = total * total + wkv[:rows] * wkv[:rows] + wkv[rows:] * wkv[rows:]
    squared = jnp.sum(jnp.sum(squared, axis=1, keepdims=True), axis=0, keepdims=True)
    squares_ref[...] = jnp.broadcast_to(squared[None], squares_ref.shape)


def finish_sums(raw, wkv):
    return pl.pallas_call(
        finish_sums_kernel,
        out_shape=[
            jax.ShapeDtypeStruct(raw.shape[1:], F32),
            jax.ShapeDtypeStruct((DP * CHIPS * 2, 1, 128), F32),
        ],
        cost_estimate=pl.CostEstimate(flops=raw.size, bytes_accessed=4 * raw.size, transcendentals=0),
        name="finish_sums",
    )(raw, wkv)


def clipped_kernel(squares_ref, wq_ref, wk_ref, wv_ref, out_ref):
    squared = jnp.sum(squares_ref[...], axis=0)[:, :1]
    clip = jnp.minimum(1.0, lax.rsqrt(squared + 1e-06))
    out_ref[:, :D] = wq_ref[...] * clip
    out_ref[:, D : 2 * D] = wk_ref[...] * clip
    out_ref[:, 2 * D :] = wv_ref[...] * clip


def clipped(squares, wq, wk, wv):
    return pl.pallas_call(
        clipped_kernel,
        out_shape=jax.ShapeDtypeStruct((wq.shape[0], 3 * D), F32),
        cost_estimate=pl.CostEstimate(flops=3 * wq.size, bytes_accessed=24 * wq.size, transcendentals=0),
        name="clipped",
    )(squares, wq, wk, wv)


def exact_kernel(left_ref, right_ref, out_ref, high_ref, middle_ref, low_ref):
    @pl.when(pl.program_id(0) == 0)
    def _():
        right = right_ref[...]
        high = right.astype(BF16)
        rest = right - high.astype(F32)
        middle = rest.astype(BF16)
        high_ref[...] = high
        middle_ref[...] = middle
        low_ref[...] = (rest - middle.astype(F32)).astype(BF16)

    left = left_ref[...]
    total = mm(left, low_ref[...], 1, 0)
    total += mm(left, middle_ref[...], 1, 0)
    out_ref[...] = total + mm(left, high_ref[...], 1, 0)


def exact_product(left, right):
    tile = 256
    return pl.pallas_call(
        exact_kernel,
        grid=(D // tile,),
        in_specs=[pl.BlockSpec((tile, D), lambda i: (i, 0)), pl.BlockSpec(right.shape, lambda i: (0, 0))],
        out_specs=pl.BlockSpec((tile, PROJ), lambda i: (i, 0)),
        out_shape=jax.ShapeDtypeStruct((D, PROJ), F32),
        scratch_shapes=[pltpu.VMEM(right.shape, BF16)] * 3,
        compiler_params=pltpu.CompilerParams(vmem_limit_bytes=32 * 1024 * 1024),
        cost_estimate=pl.CostEstimate(flops=1, bytes_accessed=1, transcendentals=0),
        name="exact_product",
    )(left, right)


def along_seq(x, dy, dz):
    return lax.ppermute(x, SEQ, moved(dy, dz, 0))


def per_device(tokens, w_query, w_key, w_value, proj_keys, proj_values, grad_out):
    inputs = tokens[0]
    upstream = grad_out[0]
    length = inputs.shape[0]
    seq_place, dp_place = lax.axis_index(SEQ), lax.axis_index("dp")
    core, chip = seq_place % 2, seq_place // 2
    y_place, z_place = chip // 4, chip % 4
    first_core = core == 0
    core_ref = core.reshape(1).astype(jnp.int32)
    rows = D // (DP * CHIPS * 2)
    quarter = CHIPS * rows
    pick = lambda x, at, axis: lax.dynamic_index_in_dim(x, at, axis, keepdims=False)

    theirs = jnp.where(first_core, proj_values, proj_keys)
    ours = jnp.where(first_core, proj_keys, proj_values)
    arrived = swap_cores(dot_f32("ps,sd->pd", theirs, inputs))
    part = dot_f32("ps,sd->pd", ours, inputs) + arrived
    raw = scatter_rows(part)

    upstream_t = upstream.T
    split = inputs.T.reshape(DP, CHIPS, 2, rows, length)
    mine = pick(split, core, 2).reshape(DP, quarter, length)
    other = pick(split, 1 - core, 2).reshape(DP, quarter, length)
    tokens_mine = [pick(mine, (dp_place + k) % DP, 0) for k in range(DP)]
    tokens_other = lax.dynamic_slice_in_dim(jnp.concatenate([other, other], axis=0), dp_place, DP, 0)
    tokens_other = tokens_other.reshape(DP * quarter, length)
    raw, upstream_t, tokens_mine, tokens_other = beside(raw, upstream_t, tokens_mine, tokens_other)
    my_tokens = gather_sum(raw)
    my_weight = jnp.where(first_core, w_key, w_value)
    query_t = dot_f32("sd,de->es", inputs, w_query).astype(BF16)
    my_tokens, my_weight, query_t, pk_t, pv_t = beside(my_tokens, my_weight, query_t, proj_keys.T, proj_values.T)
    my_proj_t = dot_f32("pe,ed->dp", my_tokens, my_weight.astype(F32), lax.Precision.HIGHEST)
    other_proj_t = swap_cores(my_proj_t)

    attended, grad_query, ours_t, theirs_t = attention(core_ref, query_t, upstream_t, my_proj_t, other_proj_t)

    part = ours_t + swap_cores(theirs_t)
    part, theirs = lax.optimization_barrier((part, dot_f32("cs,se->ce", tokens_other, grad_query)))
    raw = scatter_rows(part)
    arrived = swap_cores(theirs)
    wq = [
        dot_f32("cs,se->ce", tokens_mine[k], grad_query) + arrived[k * quarter : (k + 1) * quarter]
        for k in range(DP)
    ]
    half = quarter // 2
    up, down = along_x(wq[2][:half], 1), along_x(wq[2][half:], -1)
    ahead = jnp.concatenate([wq[1][:half] + up, wq[1][half:]], axis=0)
    behind = jnp.concatenate([wq[3][:half], wq[3][half:] + down], axis=0)
    raw, ahead, behind = beside(raw, ahead, behind)
    my_grad_t = gather_sum(raw)
    direct = dot_f32("se,de->sd", grad_query, w_query)
    columns = pick(my_tokens.reshape(PROJ, DP, CHIPS, 2 * rows), chip, 2)
    columns = jnp.concatenate([pick(columns, (dp_place + k) % DP, 1) for k in range(DP)], axis=1)
    wq = wq[0] + along_x(ahead, 1) + along_x(behind, -1)
    my_grad_t, wq, direct, columns = beside(my_grad_t, wq, direct, columns)

    raw = scatter_rows(wq)
    wkv = dot_f32("pc,ep->ce", columns, my_grad_t, lax.Precision.HIGHEST).reshape(DP, 2 * rows, D)
    wkv = wkv[0] + along_x(wkv[1], 1) + along_x(wkv[2], 2) + along_x(wkv[3], 3)
    my_grad_tokens_t = exact_product(my_weight, my_grad_t)
    raw, wkv, my_grad_tokens_t = beside(raw, wkv, my_grad_tokens_t)

    wq, squares = finish_sums(raw, wkv)
    squares = lax.all_to_all(squares, ("dp", SEQ), 0, 0)
    other_grad_tokens_t = swap_cores(my_grad_tokens_t)
    grad_tokens = finish_tokens(core_ref, direct, pk_t, pv_t, my_grad_tokens_t, other_grad_tokens_t)
    low, high = wkv[:rows], wkv[rows:]
    mine = jnp.where(first_core, low, high)
    arrived = swap_cores(jnp.where(first_core, high, low))
    wk = jnp.where(first_core, mine, arrived)
    wv = jnp.where(first_core, arrived, mine)
    squares, wk, wv, grad_tokens = beside(squares, wk, wv, grad_tokens)
    return (attended[None], grad_tokens[None], clipped(squares, wq, wk, wv))


def solution(mesh):
    return jax.shard_map(
        per_device,
        mesh=mesh,
        in_specs=(
            P("dp", "seq", None),
            P(),
            P(),
            P(),
            P(None, "seq"),
            P(None, "seq"),
            P("dp", "seq", None),
        ),
        out_specs=(P("dp", "seq", None), P("dp", "seq", None), P(("dp", "seq"), None)),
        check_vma=False,
    )
```

```python
import functools

import jax
import jax.numpy as jnp
from jax import lax
from jax.experimental import pallas as pl
from jax.experimental.pallas import tpu as pltpu
from jax.sharding import PartitionSpec as P

D = 1024
HEADS = 16
HEAD_DIM = 64
PROJ = 256
DP = 4
CHIPS = 16
SEQ = "seq"
F32 = jnp.float32
BF16 = jnp.bfloat16
GROUP = 4
LOG2E = 1.4426950408889634


def place(y, z, core):
    return ((y % 4) * 4 + z % 4) * 2 + core % 2


def moved(dy, dz, dcore):
    return [
        (place(y, z, c), place(y + dy, z + dz, c + dcore))
        for y in range(4)
        for z in range(4)
        for c in range(2)
    ]


SAME_CORE = [[2 * chip + core for chip in range(CHIPS)] for core in range(2)]


def swap_cores(x):
    return lax.ppermute(x, SEQ, moved(0, 0, 1))


def along_x(x, step):
    return lax.ppermute(x, "dp", [(d, (d + step) % DP) for d in range(DP)])


def exchange_chips(x):
    return lax.all_to_all(x, SEQ, 0, 0, axis_index_groups=SAME_CORE)


def beside(x, *others):
    return lax.optimization_barrier((x, *others))


def scatter_rows(x):
    return exchange_chips(x.reshape(CHIPS, x.shape[0] // CHIPS, x.shape[1]))


def gather_sum(raw):
    copies = sum_copies(raw)
    rows = exchange_chips(copies)
    return rows.reshape(raw.shape[0] * raw.shape[1], raw.shape[2])


def dot_f32(form, left, right, precision=None):
    return jnp.einsum(form, left, right, preferred_element_type=F32, precision=precision)


def mm(left, right, left_dim, right_dim):
    return lax.dot_general(
        left, right, (((left_dim,), (right_dim,)), ((), ())), preferred_element_type=F32
    )


def attention_kernel(core_ref, query_ref, grad_ref, mine_ref, other_ref, att_ref, gq_ref, ours_ref, theirs_ref):
    first_core = core_ref[0] == 0
    mine, other = mine_ref[...], other_ref[...]
    keys = jnp.where(first_core, mine, other).astype(BF16)
    values = jnp.where(first_core, other, mine).astype(BF16)
    att, gq, gk, gv = [], [], [], []
    for h in range(GROUP):
        rows = slice(h * HEAD_DIM, (h + 1) * HEAD_DIM)
        query, grad, key, value = query_ref[rows, :], grad_ref[rows, :], keys[rows], values[rows]
        scores = mm(key, query, 0, 0)
        top = jnp.max(scores, axis=0, keepdims=True)
        raised = jnp.exp2((scores - top) * (0.125 * LOG2E))
        probs = raised * (1.0 / jnp.sum(raised, axis=0, keepdims=True))
        low = probs.astype(BF16)
        dprobs = mm(value * BF16(0.125), grad, 0, 0)
        inner = jnp.sum(dprobs * probs, axis=0, keepdims=True)
        dscores = (probs * (dprobs - inner)).astype(BF16)
        att.append(mm(value, low, 1, 0))
        gq.append(mm(key, dscores, 1, 0))
        gk.append(mm(query, dscores, 1, 1))
        gv.append(mm(grad, low, 1, 1))
    att_ref[...] = jnp.concatenate(att, axis=0).T.astype(BF16)
    gq_ref[...] = jnp.concatenate(gq, axis=0).T.astype(BF16)
    gk, gv = jnp.concatenate(gk, axis=0), jnp.concatenate(gv, axis=0)
    ours_ref[...] = jnp.where(first_core, gk, gv)
    theirs_ref[...] = jnp.where(first_core, gv, gk)


def attention(core, query_t, grad_t, mine_t, other_t):
    length = query_t.shape[1]
    wide = pl.BlockSpec((GROUP * HEAD_DIM, length), lambda i: (i, 0))
    narrow = pl.BlockSpec((GROUP * HEAD_DIM, PROJ), lambda i: (i, 0))
    tall = pl.BlockSpec((length, GROUP * HEAD_DIM), lambda i: (0, i))
    return pl.pallas_call(
        attention_kernel,
        grid=(HEADS // GROUP,),
        in_specs=[pl.BlockSpec(memory_space=pltpu.SMEM), wide, wide, narrow, narrow],
        out_specs=[tall, tall, narrow, narrow],
        out_shape=[
            jax.ShapeDtypeStruct((length, D), BF16),
            jax.ShapeDtypeStruct((length, D), BF16),
            jax.ShapeDtypeStruct((D, PROJ), F32),
            jax.ShapeDtypeStruct((D, PROJ), F32),
        ],
        compiler_params=pltpu.CompilerParams(vmem_limit_bytes=48 * 1024 * 1024),
        cost_estimate=pl.CostEstimate(
            flops=12 * length * PROJ * D, bytes_accessed=8 * 1024 * 1024, transcendentals=length * PROJ * HEADS
        ),
        name="attention",
    )(core, query_t, grad_t, mine_t, other_t)


def sum_copies_kernel(x_ref, out_ref):
    total = x_ref[0]
    for chip in range(1, CHIPS):
        total += x_ref[chip]
    for chip in range(CHIPS):
        out_ref[chip] = total


def sum_copies(x):
    return pl.pallas_call(
        sum_copies_kernel,
        out_shape=jax.ShapeDtypeStruct(x.shape, F32),
        cost_estimate=pl.CostEstimate(flops=x.size, bytes_accessed=8 * x.size, transcendentals=0),
        compiler_params=pltpu.CompilerParams(vmem_limit_bytes=32 * 1024 * 1024),
        name="sum_copies",
    )(x)


def grad_tokens_kernel(core_ref, first_ref, pk_ref, pv_ref, mine_ref, other_ref, out_ref):
    first_core = core_ref[0] == 0
    mine, other = mine_ref[...], other_ref[...]
    gk = jnp.where(first_core, mine, other).astype(BF16)
    gv = jnp.where(first_core, other, mine).astype(BF16)
    total = first_ref[...]
    total += mm(pk_ref[...], gk, 1, 1)
    total += mm(pv_ref[...], gv, 1, 1)
    out_ref[...] = total.astype(BF16)


def finish_tokens(core, first, pk_t, pv_t, mine_t, other_t):
    length = first.shape[0]
    tile = 256
    column = pl.BlockSpec((length, tile), lambda i: (0, i))
    row = pl.BlockSpec((tile, PROJ), lambda i: (i, 0))
    whole = pl.BlockSpec((length, PROJ), lambda i: (0, 0))
    return pl.pallas_call(
        grad_tokens_kernel,
        grid=(D // tile,),
        in_specs=[pl.BlockSpec(memory_space=pltpu.SMEM), column, whole, whole, row, row],
        out_specs=column,
        out_shape=jax.ShapeDtypeStruct((length, D), BF16),
        compiler_params=pltpu.CompilerParams(vmem_limit_bytes=56 * 1024 * 1024),
        cost_estimate=pl.CostEstimate(
            flops=1, bytes_accessed=1, transcendentals=0
        ),
        name="grad_tokens",
    )(core, first, pk_t, pv_t, mine_t, other_t)


def exchange_x(x):
    return lax.all_to_all(x, "dp", 0, 0)


def finish_sums_kernel(raw_ref, wkv_ref, wq_ref, squares_ref):
    total = raw_ref[0]
    for chip in range(1, CHIPS):
        total += raw_ref[chip]
    wq_ref[...] = total
    wkv = wkv_ref[...]
    rows = total.shape[0]
    squared = total * total + wkv[:rows] * wkv[:rows] + wkv[rows:] * wkv[rows:]
    squared = jnp.sum(jnp.sum(squared, axis=1, keepdims=True), axis=0, keepdims=True)
    squares_ref[...] = jnp.broadcast_to(squared[None], squares_ref.shape)


def finish_sums(raw, wkv):
    return pl.pallas_call(
        finish_sums_kernel,
        out_shape=[
            jax.ShapeDtypeStruct(raw.shape[1:], F32),
            jax.ShapeDtypeStruct((DP * CHIPS * 2, 1, 128), F32),
        ],
        cost_estimate=pl.CostEstimate(flops=raw.size, bytes_accessed=4 * raw.size, transcendentals=0),
        name="finish_sums",
    )(raw, wkv)


def clipped_kernel(core_ref, squares_ref, wq_ref, wkv_ref, arrived_ref, out_ref):
    first_core = core_ref[0] == 0
    rows = wq_ref.shape[0]
    squared = jnp.sum(squares_ref[...], axis=0)[:, :1]
    clip = jnp.minimum(1.0, lax.rsqrt(squared + 1e-06))
    mine = jnp.where(first_core, wkv_ref[:rows], wkv_ref[rows:]) * clip
    arrived = arrived_ref[...] * clip
    out_ref[:, :D] = wq_ref[...] * clip
    out_ref[:, D : 2 * D] = jnp.where(first_core, mine, arrived)
    out_ref[:, 2 * D :] = jnp.where(first_core, arrived, mine)


def clipped(core, squares, wq, wkv, arrived):
    whole = pl.BlockSpec(memory_space=pltpu.VMEM)
    return pl.pallas_call(
        clipped_kernel,
        in_specs=[pl.BlockSpec(memory_space=pltpu.SMEM), whole, whole, whole, whole],
        out_specs=whole,
        out_shape=jax.ShapeDtypeStruct((wq.shape[0], 3 * D), F32),
        cost_estimate=pl.CostEstimate(flops=3 * wq.size, bytes_accessed=24 * wq.size, transcendentals=0),
        name="clipped",
    )(core, squares, wq, wkv, arrived)


def exact_kernel(left_ref, right_ref, out_ref, high_ref, middle_ref, low_ref):
    @pl.when(pl.program_id(0) == 0)
    def _():
        right = right_ref[...]
        high = right.astype(BF16)
        rest = right - high.astype(F32)
        middle = rest.astype(BF16)
        high_ref[...] = high
        middle_ref[...] = middle
        low_ref[...] = (rest - middle.astype(F32)).astype(BF16)

    left = left_ref[...]
    total = mm(left, low_ref[...], 1, 0)
    total += mm(left, middle_ref[...], 1, 0)
    out_ref[...] = total + mm(left, high_ref[...], 1, 0)


def exact_product(left, right):
    tile = 256
    return pl.pallas_call(
        exact_kernel,
        grid=(D // tile,),
        in_specs=[pl.BlockSpec((tile, D), lambda i: (i, 0)), pl.BlockSpec(right.shape, lambda i: (0, 0))],
        out_specs=pl.BlockSpec((tile, PROJ), lambda i: (i, 0)),
        out_shape=jax.ShapeDtypeStruct((D, PROJ), F32),
        scratch_shapes=[pltpu.VMEM(right.shape, BF16)] * 3,
        compiler_params=pltpu.CompilerParams(vmem_limit_bytes=32 * 1024 * 1024),
        cost_estimate=pl.CostEstimate(flops=1, bytes_accessed=1, transcendentals=0),
        name="exact_product",
    )(left, right)


def along_seq(x, dy, dz):
    return lax.ppermute(x, SEQ, moved(dy, dz, 0))


def per_device(tokens, w_query, w_key, w_value, proj_keys, proj_values, grad_out):
    inputs = tokens[0]
    upstream = grad_out[0]
    length = inputs.shape[0]
    seq_place, dp_place = lax.axis_index(SEQ), lax.axis_index("dp")
    core, chip = seq_place % 2, seq_place // 2
    y_place, z_place = chip // 4, chip % 4
    first_core = core == 0
    core_ref = core.reshape(1).astype(jnp.int32)
    rows = D // (DP * CHIPS * 2)
    quarter = CHIPS * rows
    pick = lambda x, at, axis: lax.dynamic_index_in_dim(x, at, axis, keepdims=False)

    theirs = jnp.where(first_core, proj_values, proj_keys)
    ours = jnp.where(first_core, proj_keys, proj_values)
    arrived = swap_cores(dot_f32("ps,sd->pd", theirs, inputs))
    part = dot_f32("ps,sd->pd", ours, inputs) + arrived
    raw = scatter_rows(part)

    upstream_t = upstream.T
    split = inputs.T.reshape(DP, CHIPS, 2, rows, length)
    mine = pick(split, core, 2).reshape(DP, quarter, length)
    other = pick(split, 1 - core, 2).reshape(DP, quarter, length)
    tokens_mine = [pick(mine, (dp_place + k) % DP, 0) for k in range(DP)]
    tokens_other = lax.dynamic_slice_in_dim(jnp.concatenate([other, other], axis=0), dp_place, DP, 0)
    tokens_other = tokens_other.reshape(DP * quarter, length)
    raw, upstream_t, tokens_mine, tokens_other = beside(raw, upstream_t, tokens_mine, tokens_other)
    my_tokens = gather_sum(raw)
    my_weight = jnp.where(first_core, w_key, w_value)
    query_t = dot_f32("sd,de->es", inputs, w_query).astype(BF16)
    my_tokens, my_weight, query_t, pk_t, pv_t = beside(my_tokens, my_weight, query_t, proj_keys.T, proj_values.T)
    my_proj_t = dot_f32("pe,ed->dp", my_tokens, my_weight.astype(F32), lax.Precision.HIGHEST)
    other_proj_t = swap_cores(my_proj_t)

    attended, grad_query, ours_t, theirs_t = attention(core_ref, query_t, upstream_t, my_proj_t, other_proj_t)

    part = ours_t + swap_cores(theirs_t)
    part, theirs = lax.optimization_barrier((part, dot_f32("cs,se->ce", tokens_other, grad_query)))
    raw = scatter_rows(part)
    arrived = swap_cores(theirs)
    wq = [
        dot_f32("cs,se->ce", tokens_mine[k], grad_query) + arrived[k * quarter : (k + 1) * quarter]
        for k in range(DP)
    ]
    my_tokens, wq[3] = lax.optimization_barrier((my_tokens, wq[3]))
    columns = pick(my_tokens.reshape(PROJ, DP, CHIPS, 2 * rows), chip, 2)
    columns = jnp.concatenate([pick(columns, (dp_place + k) % DP, 1) for k in range(DP)], axis=1)
    half = quarter // 2
    up, down = along_x(wq[2][:half], 1), along_x(wq[2][half:], -1)
    ahead = jnp.concatenate([wq[1][:half] + up, wq[1][half:]], axis=0)
    behind = jnp.concatenate([wq[3][:half], wq[3][half:] + down], axis=0)
    raw, ahead, behind, columns = beside(raw, ahead, behind, columns)
    my_grad_t = gather_sum(raw)
    direct = dot_f32("se,de->sd", grad_query, w_query)
    wq = wq[0] + along_x(ahead, 1) + along_x(behind, -1)
    my_grad_t, wq, direct = beside(my_grad_t, wq, direct)

    raw = scatter_rows(wq)
    wkv = dot_f32("pc,ep->ce", columns, my_grad_t, lax.Precision.HIGHEST).reshape(DP, 2 * rows, D)
    wkv = wkv[0] + along_x(wkv[1], 1) + along_x(wkv[2], 2) + along_x(wkv[3], 3)
    my_grad_tokens_t = exact_product(my_weight, my_grad_t)
    raw, wkv, my_grad_tokens_t = beside(raw, wkv, my_grad_tokens_t)

    wq, squares = finish_sums(raw, wkv)
    squares = lax.all_to_all(squares, ("dp", SEQ), 0, 0)
    other_grad_tokens_t = swap_cores(my_grad_tokens_t)
    grad_tokens = finish_tokens(core_ref, direct, pk_t, pv_t, my_grad_tokens_t, other_grad_tokens_t)
    arrived = swap_cores(jnp.where(first_core, wkv[rows:], wkv[:rows]))
    squares, arrived, grad_tokens = beside(squares, arrived, grad_tokens)
    return (attended[None], grad_tokens[None], clipped(core_ref, squares, wq, wkv, arrived))


def solution(mesh):
    return jax.shard_map(
        per_device,
        mesh=mesh,
        in_specs=(
            P("dp", "seq", None),
            P(),
            P(),
            P(),
            P(None, "seq"),
            P(None, "seq"),
            P("dp", "seq", None),
        ),
        out_specs=(P("dp", "seq", None), P("dp", "seq", None), P(("dp", "seq"), None)),
        check_vma=False,
    )
```
